256 devices in a mesh: ctx: 16 (over y, x), exp: 16 (over z, core).
Axes of the slice: x: 4, y: 4, z: 8, core: 2. Of those that a mesh axis runs over, the one named last changes fastest.
Arguments:
- tokens: bfloat16 [32768, 2048], P(('ctx', 'exp')), may hold values from -6 to 6
- expert_ids: int32 [32768, 8], P(('ctx', 'exp')), may hold values from 0 to 127, all different within a row; in each aligned block of 128 rows (0 to 127, 128 to 255, ...) at most 10 rows name the same one
- gate_probs: float32 [32768, 8], P(('ctx', 'exp')), may hold values from 0.05 to 1
- w_gate: bfloat16 [256, 2048, 384], P(('ctx', 'exp')), may hold values from -0.125 to 0.125
- w_up: bfloat16 [256, 2048, 384], P(('ctx', 'exp')), may hold values from -0.125 to 0.125
- w_down: bfloat16 [256, 384, 2048], P(('ctx', 'exp')), may hold values from -0.21875 to 0.21875
Outputs:
- mixed: bfloat16 [32768, 2048], P(('ctx', 'exp'))
The draws below stay inside these ranges and needn't reach their ends.
Inputs may be any that keep to these rules, and one draw needn't show every extreme that they name: `expert_ids`: each row names 8 different experts. Among the 128 rows of one device no expert is named by more than 10 rows, a bound that some block reaches.
All inputs are finite; a program needn't handle non-finite values.
Results may differ from the reference program's by a relative error of at most 0.0065.
Values may be sent and summed in bfloat16 or wider, within the bound.
A program may use at most 128 MiB of HBM per device.

```python
import math
import jax
import jax.numpy as jnp
import numpy as np
from jax import lax

D = 2048
FF = 768
TOP = 8
TOK_DEV = 128
EXPERTS = 128
TOKENS = 32768
CAP = 10
HALF = 384
N_CTX = 16
N_EXP = 16


def shard_levels(stream_key, dims, pieces, least, top_value):
    def one(dim, shards_of):
        heights = jax.random.uniform(jax.random.fold_in(jax.random.fold_in(stream_key, 6), dim), (shards_of,), jnp.float32, least / len(pieces), top_value / len(pieces))
        return jnp.repeat(jnp.exp(heights), dims[dim] // shards_of).reshape((-1,) + (1,) * (len(dims) - dim - 1))

    gain = one(*pieces[0])
    for cut in pieces[1:]:
        gain = gain * one(*cut)
    return gain


def assign_block(stream_key, own, number, rows, count, top, limit, skew):
    order = jax.random.permutation(stream_key, count)
    crowded, usual = load_shares(count, rows * top, limit, skew, True), load_shares(count, rows * top, limit, skew, False)
    places = jnp.arange(count)

    def named(sizes, turn):
        used = int((sizes > 0).sum())
        fixed = max(1, used // 4)
        passed = fixed + (places - fixed + turn * (used - fixed)) % max(1, count - fixed)
        return jnp.zeros((count,), jnp.int32).at[order[jnp.where(places < fixed, places, passed)]].set(jnp.asarray(sizes, jnp.int32))

    sizes = jnp.where(number % 4 == 0, named(crowded, number // 4), named(usual, number - number // 4 - 1))
    mixed = jax.random.permutation(jax.random.fold_in(own, 3), count)
    giver, receiver = mixed[0:count // 2 * 2:2], mixed[1:count // 2 * 2:2]
    room = jnp.minimum(sizes[giver] - 1, limit - sizes[receiver]) // 2
    room = jnp.where((giver == order[0]) | (receiver == order[0]) | (sizes[receiver] == 0), 0, jnp.maximum(room, 0))
    passed = jax.random.randint(jax.random.fold_in(own, 4), (count // 2,), 0, 1 << 20) % (room + 1)
    sizes = sizes.at[giver].add(-passed).at[receiver].add(passed)
    items = jnp.searchsorted(jnp.cumsum(sizes), jnp.arange(rows * top), side="right").astype(jnp.int32)
    table = items.reshape(top, rows).T
    table = table[jax.random.permutation(jax.random.fold_in(own, 1), rows)]
    turn = jax.random.randint(jax.random.fold_in(own, 2), (rows, 1), 0, top)
    return jnp.take_along_axis(table, (jnp.arange(top)[None, :] + turn) % top, axis=1)


def load_shares(count, total, bound, lean, full):
    portions = [(1 << 20) // math.isqrt(rank ** lean) + 1 for rank in range(1, count + 1)]
    largest = bound if full else min(bound, max(-(-total // count), total * portions[0] // sum(portions)))
    least = 1 if total - largest >= count - 1 else 0
    given, rest = [largest] + [least] * (count - 1), total - largest - least * (count - 1)
    while rest > 0:
        candidates = [i for i in range(1, count) if given[i] < largest] or [i for i in range(1, count) if given[i] < bound]
        mass, budget = sum([portions[i] for i in candidates]), rest
        for i in candidates:
            more = min(bound - given[i], max(1, budget * portions[i] // mass), rest)
            given[i] = given[i] + more
            rest = rest - more
    return np.array(given)


def scatter_about(stream_key, extent, scale, most, split=(), kind=jnp.bfloat16):
    entries = scale * jax.random.normal(stream_key, extent, jnp.float32)
    if split:
        entries = entries * shard_levels(stream_key, extent, split, -0.22, 0.18)
    return jnp.clip(entries, -most, most).astype(kind)


def setup_inputs(seed: int = 0) -> dict:
    streams_of = jax.random.split(jax.random.key(seed), 7)
    tokens = scatter_about(streams_of[0], (TOKENS, D), 1.0, 6.0, ((0, 256),))
    expert_ids_keys = jax.random.split(jax.random.fold_in(streams_of[1], 1), TOKENS // TOK_DEV)
    expert_ids_turns = jax.random.permutation(jax.random.fold_in(streams_of[1], 3), TOKENS // TOK_DEV)
    expert_ids = jax.vmap(lambda own, number: assign_block(jax.random.fold_in(streams_of[1], 2), own, number, TOK_DEV, EXPERTS, TOP, CAP, 1))(expert_ids_keys, expert_ids_turns).reshape((TOKENS, TOP))
    gate_probs = jnp.clip(jnp.exp(math.log(1.0) - 2.9957323 * jax.random.uniform(streams_of[2], (TOKENS, TOP), jnp.float32) ** shard_levels(streams_of[2], (TOKENS, TOP), ((0, 256),), -0.2, 0.2)), 0.05, 1.0)
    w_gate = scatter_about(streams_of[3], (2 * EXPERTS, D, HALF), D ** -0.5, 0.125, ((0, 256),))
    w_up = scatter_about(streams_of[4], (2 * EXPERTS, D, HALF), D ** -0.5, 0.125, ((0, 256),))
    w_down = scatter_about(streams_of[5], (2 * EXPERTS, HALF, D), FF ** -0.5, 0.21875, ((0, 256),))
    return {"tokens": tokens, "expert_ids": expert_ids, "gate_probs": gate_probs, "w_gate": w_gate, "w_up": w_up, "w_down": w_down}


def expert_rows(row_block, gate_pair, up_pair, down_pair):
    summed = jnp.zeros((row_block.shape[0], down_pair.shape[2]), jnp.float32)
    for half_index in range(2):
        gate_sum = jnp.dot(row_block, gate_pair[half_index].astype(jnp.float32), precision=lax.Precision.HIGHEST)
        up_sum = jnp.dot(row_block, up_pair[half_index].astype(jnp.float32), precision=lax.Precision.HIGHEST)
        hidden = lax.optimization_barrier((jax.nn.silu(gate_sum) * up_sum).astype(jnp.bfloat16))
        partial_value = jnp.dot(hidden.astype(jnp.float32), down_pair[half_index].astype(jnp.float32), precision=lax.Precision.HIGHEST)
        partial_value = lax.optimization_barrier(partial_value.astype(jnp.bfloat16))
        summed = summed + partial_value.astype(jnp.float32)
    return summed.astype(jnp.bfloat16)


def reference(tokens, expert_ids, gate_probs, w_gate, w_up, w_down):
    devices_all = N_CTX * N_EXP
    weights = gate_probs / jnp.sum(gate_probs, axis=1, keepdims=True)
    id_blocks = expert_ids.reshape(devices_all, TOK_DEV * TOP)

    def rank_of(id_block):
        matches = (id_block[:, None] == jnp.arange(EXPERTS, dtype=jnp.int32)[None, :]).astype(jnp.int32)
        earlier = jnp.cumsum(matches, axis=0) - matches
        return jnp.sum(earlier * matches, axis=1).astype(jnp.int32)

    slot_rank = lax.map(rank_of, id_blocks)
    device_of = jnp.broadcast_to(jnp.arange(devices_all, dtype=jnp.int32)[:, None], id_blocks.shape)
    local_of = jnp.broadcast_to(jnp.arange(TOK_DEV * TOP, dtype=jnp.int32)[None, :], id_blocks.shape)
    token_of = (device_of * TOK_DEV + local_of // TOP).astype(jnp.int32)
    table = jnp.full((EXPERTS, devices_all, CAP), TOKENS, jnp.int32).at[id_blocks, device_of, slot_rank].set(token_of)
    shares = jnp.zeros((EXPERTS, devices_all, CAP), jnp.float32).at[id_blocks, device_of, slot_rank].set(weights.reshape(devices_all, TOK_DEV * TOP))
    padded = jnp.concatenate([tokens, jnp.zeros((1, D), jnp.bfloat16)], axis=0)
    gates = w_gate.reshape(EXPERTS, 2, D, HALF)
    ups = w_up.reshape(EXPERTS, 2, D, HALF)
    downs = w_down.reshape(EXPERTS, 2, HALF, D)

    def per_expert(summed, scanned):
        row_index, row_share, gate_pair, up_pair, down_pair = scanned
        row_index = row_index.reshape(-1)
        row_block = padded[row_index].astype(jnp.float32)
        result = expert_rows(row_block, gate_pair, up_pair, down_pair)
        summed = summed.at[row_index].add(row_share.reshape(-1)[:, None] * result.astype(jnp.float32))
        return summed, None

    summed, unused = lax.scan(per_expert, jnp.zeros((TOKENS + 1, D), jnp.float32), (table, shares, gates, ups, downs))
    return summed[:TOKENS].astype(jnp.bfloat16)
```

```python
import functools

import jax
import jax.numpy as jnp
from jax import lax
from jax.experimental import pallas as pl
from jax.experimental.pallas import tpu as pltpu
from jax.sharding import PartitionSpec as P

MESH = pl.DeviceIdType.MESH
F32 = jnp.float32
BF16 = jnp.bfloat16

NY, NX, NZ = 4, 4, 8
PEERS = NY * NX
CAP = 10
ROWS = NZ * CAP
ALL = PEERS * ROWS
GATHER_AHEAD = 2
SEND_AHEAD = 2
RETURN_AHEAD = 2
GROUP = 4
SUMS = 6
ORDER = (1, 4, 3, 12, 2, 8, 5, 15, 7, 13, 6, 9, 14, 11, 10)


def kernel(
    tok, meta, w_gate, w_up, w_down, out,
    ring, metas, pick, spread, place, share, packed, came, w_in, w_out, acc, hidden, back, part, sums,
    tok_sem, meta_s, meta_r, wt_l, wt_s, wt_r, ring_s, ring_r, row_s, row_r, back_r, sum_s, sum_r,
):
    n_tok, d = tok.shape
    chunks, _, width = ring.shape
    half = w_down.shape[1]
    tiles = w_in.shape[1] // 256
    block = GROUP * ROWS
    ctx, exp = lax.axis_index("ctx"), lax.axis_index("exp")
    y, x = ctx // NX, lax.rem(ctx, NX)
    z, core = exp // 2, lax.rem(exp, 2)

    def up(j):
        return (ctx, lax.rem(z + j, NZ) * 2 + core)

    def ahead(i):
        return (lax.rem(y + i // NX, NY) * NX + lax.rem(x + i % NX, NX), exp)

    def behind(i):
        return (lax.rem(y + NY - i // NX, NY) * NX + lax.rem(x + NX - i % NX, NX), exp)

    sibling = (ctx, z * 2 + 1 - core)

    def rdma(src, dst, send, recv, to):
        return pltpu.make_async_remote_copy(
            src_ref=src, dst_ref=dst, send_sem=send, recv_sem=recv, device_id=to, device_id_type=MESH
        )

    def token_rows(j):
        return pl.ds(pl.multiple_of(j * n_tok, n_tok), n_tok)

    def peer_rows(i):
        return pl.ds(pl.multiple_of(i * ROWS, ROWS), ROWS)

    def columns(f):
        return pl.ds(pl.multiple_of(f * width, width), width)

    def own_tokens(f):
        return pltpu.make_async_copy(tok.at[:, columns(f)], ring.at[f, token_rows(0)], tok_sem.at[f])

    for f in range(chunks):
        own_tokens(f).start()
    weight_parts = (
        (w_gate.at[0], w_in, (pl.ds(0, d), 0, half)),
        (w_up.at[0], w_in, (pl.ds(0, d), 2 * half, half)),
        (w_down.at[0], w_out, (None, 0, half)),
    )

    def weight_dst(k, other):
        _, ref, (rows, at, size) = weight_parts[k]
        at = at + other * half
        if rows is None:
            return ref.at[pl.ds(at, size)]
        return ref.at[rows, pl.ds(at, size)]

    def weight_local(k):
        return pltpu.make_async_copy(weight_parts[k][0], weight_dst(k, 0), wt_l.at[k])

    def weight_remote(k):
        return rdma(weight_parts[k][0], weight_dst(k, 1), wt_s.at[k], wt_r.at[k], sibling)

    barrier = pltpu.get_barrier_semaphore()
    for j in range(1, NZ):
        pl.semaphore_signal(barrier, inc=1, device_id=up(j), device_id_type=MESH)
    for i in range(1, PEERS):
        pl.semaphore_signal(barrier, inc=1, device_id=ahead(i), device_id_type=MESH)
    pl.semaphore_signal(barrier, inc=1, device_id=sibling, device_id_type=MESH)
    metas[0] = meta[...]
    pl.semaphore_wait(barrier, NZ + PEERS - 1)

    def meta_copy(j):
        return rdma(meta, metas.at[j], meta_s.at[j], meta_r.at[j], up(NZ - j))

    def ring_copy(f, src, dst, to):
        return rdma(ring.at[f, token_rows(src)], ring.at[f, token_rows(dst)], ring_s.at[f, dst], ring_r.at[f, dst], to)

    def ring_wait(f, j):
        ring_copy(f, j, j, up(1)).wait_recv()

    def gather_start(f):
        own_tokens(f).wait()
        ring_copy(f, 0, 7, up(1)).start()
        ring_copy(f, 0, 1, up(NZ - 1)).start()

    def gather_second(f):
        ring_wait(f, 7)
        ring_copy(f, 7, 6, up(1)).start()
        ring_wait(f, 1)
        ring_copy(f, 1, 2, up(NZ - 1)).start()

    def gather_third(f):
        ring_wait(f, 6)
        ring_copy(f, 6, 5, up(1)).start()
        ring_wait(f, 2)
        ring_copy(f, 2, 3, up(NZ - 1)).start()

    def gather_fourth(f):
        odd = lax.rem(f, 2)
        ring_wait(f, 5)
        ring_wait(f, 3)
        ring_copy(f, 5 - 2 * odd, 4, up(1 + (NZ - 2) * odd)).start()

    def gather_last(f):
        ring_wait(f, 4)

    def build_places():
        for j in range(1, NZ):
            meta_copy(j).wait_recv()
        i = lax.broadcasted_iota(jnp.int32, (PEERS, n_tok), 0)
        row, col = lax.shift_right_logical(i, 2) + y, lax.bitwise_and(i, 3) + x
        owner = lax.bitwise_and(row, 3) * NX + lax.bitwise_and(col, 3)
        expert = (owner * NZ + z).astype(F32)
        earlier = (
            lax.broadcasted_iota(jnp.int32, (n_tok, n_tok), 0) < lax.broadcasted_iota(jnp.int32, (n_tok, n_tok), 1)
        ).astype(F32).astype(BF16)
        for j in range(NZ):
            named = jnp.zeros((PEERS, n_tok), F32)
            weight = jnp.zeros((PEERS, n_tok), F32)
            for k in range(8):
                hit = metas[j, k : k + 1, :] == expert
                named = named + jnp.where(hit, 1.0, 0.0)
                weight = weight + jnp.where(hit, metas[j, 8 + k : 9 + k, :], 0.0)
            rank = jnp.dot(named.astype(BF16), earlier, preferred_element_type=F32)
            place[:, j * n_tok : (j + 1) * n_tok] = jnp.where(named > 0.5, rank + float(j * CAP), -1.0)
            share[:, j * n_tok : (j + 1) * n_tok] = weight

        def one_peer(i, carry):
            slot = lax.broadcasted_iota(jnp.int32, (ROWS, NZ * n_tok), 0).astype(F32)
            hit = slot == place[pl.ds(i, 1), :]
            pick[peer_rows(i), :] = jnp.where(hit, 1.0, 0.0).astype(BF16)
            return carry

        lax.fori_loop(0, PEERS, one_peer, 0)

    def build_spread():
        lane = lax.broadcasted_iota(jnp.int32, (PEERS, ALL), 1)
        first = lax.broadcasted_iota(jnp.int32, (PEERS, ALL), 0) * ROWS
        inside = jnp.logical_and(lane >= first, lane < first + ROWS)
        widen = jnp.where(inside, 1.0, 0.0).astype(BF16)
        slot = jnp.sum(jnp.where(inside, (lane - first).astype(F32), 0.0), axis=0, keepdims=True)

        def one_block(j, carry):
            at = token_rows(j)
            dims = (((0,), (0,)), ((), ()))
            target = lax.dot_general(place[:, at].astype(BF16), widen, dims, preferred_element_type=F32)
            weight = lax.dot_general(share[:, at].astype(BF16), widen, dims, preferred_element_type=F32)
            spread[at, :] = jnp.where(target == slot, weight, 0.0).astype(BF16)
            return carry

        lax.fori_loop(0, NZ, one_block, 0)

    def pack(f):
        def one_block(b, carry):
            rows = pl.ds(pl.multiple_of(b * block, block), block)
            packed[f, rows, :] = jnp.dot(pick[rows, :], ring[f], preferred_element_type=F32).astype(BF16)
            return carry

        lax.fori_loop(0, PEERS // GROUP, one_block, 0)

    def row_copy(f, i):
        at = peer_rows(i)
        if i == 0:
            return pltpu.make_async_copy(packed.at[f, at], came.at[f, at], row_r.at[f, i])
        return rdma(packed.at[f, at], came.at[f, at], row_s.at[f, i], row_r.at[f, i], ahead(i))

    def send_rows(f):
        for i in ORDER + (0,):
            row_copy(f, i).start()

    def gate_up(f, b):
        for i in range(GROUP):
            at = peer_rows(b * GROUP + i)
            pltpu.make_async_copy(came.at[f, at], came.at[f, at], row_r.at[f, b * GROUP + i]).wait()
        rows = pl.ds(pl.multiple_of(b * block, block), block)
        depth = pl.ds(pl.multiple_of(f * width, width), width)
        xs = came[f, rows, :]
        for t in range(tiles):
            acc[t, rows, :] += jnp.dot(xs, w_in[depth, t * 256 : (t + 1) * 256], preferred_element_type=F32)

    def activate(b):
        for q in range(GROUP):
            rows = peer_rows(b * GROUP + q)
            for t in range(tiles // 2):
                g, u = acc[t, rows, :], acc[tiles // 2 + t, rows, :]
                hidden[rows, t * 256 : (t + 1) * 256] = (g / (1.0 + jnp.exp(-g)) * u).astype(BF16)

    def back_copy(n, i):
        at = peer_rows(i)
        if i == 0:
            return pltpu.make_async_copy(packed.at[n, at], back.at[n, at], back_r.at[n, i])
        return rdma(packed.at[n, at], back.at[n, at], row_s.at[n, i], back_r.at[n, i], behind(i))

    def rows_sent(n):
        for i in range(1, PEERS):
            row_copy(n, i).wait_send()

    def down(n, b):
        rows = pl.ds(pl.multiple_of(b * block, block), block)
        packed[n, rows, :] = jnp.dot(hidden[rows, :], w_out[:, columns(n)], preferred_element_type=F32).astype(BF16)

    def down_and_send(n):
        rows_sent(n)

        def one_block(b, carry):
            down(n, b)
            return carry

        lax.fori_loop(0, PEERS // GROUP, one_block, 0)
        for i in ORDER + (0,):
            back_copy(n, i).start()

    def sum_copy(n, slot, to):
        return rdma(part.at[n, token_rows(slot)], sums.at[n, token_rows(slot)], sum_s.at[n, slot], sum_r.at[n, slot], to)

    def total(n, j):
        return acc[lax.rem(n, SUMS), token_rows(j), :]

    def pass_on(n, j, slot_in, slot_out, to):
        value = total(n, j)
        if slot_in is not None:
            sum_copy(n, slot_in, to).wait_recv()
            value = value + sums[n, token_rows(slot_in), :].astype(F32)
        part[n, token_rows(slot_out), :] = value.astype(BF16)
        sum_copy(n, slot_out, to).start()

    def combine(n):
        for i in range(PEERS):
            at = peer_rows(i)
            pltpu.make_async_copy(back.at[n, at], back.at[n, at], back_r.at[n, i]).wait()

        def one_block(j, carry):
            acc[lax.rem(n, SUMS), token_rows(j), :] = jnp.dot(
                spread[token_rows(j), :], back[n], preferred_element_type=F32
            )
            return carry

        lax.fori_loop(0, NZ, one_block, 0)
        odd = lax.rem(n, 2)
        pass_on(n, 4 - odd, None, 3 - odd, up(1))
        pass_on(n, 5 - odd, None, 5 - odd, up(NZ - 1))

    def reduce_hop(n, k):
        odd = lax.rem(n, 2)
        j = 5 - k - odd
        pass_on(n, j, j, j - 1, up(1))
        j = 4 + k - odd
        pass_on(n, j, j - 1, j, up(NZ - 1))

    def reduce_fourth(n):
        odd = lax.rem(n, 2)
        pass_on(n, 1 + 6 * odd, 1 + 5 * odd, 7 * odd, up(1 + (NZ - 2) * odd))

    def reduce_last(n):
        value = total(n, 0)
        for slot in (0, 7):
            sum_copy(n, slot, up(1)).wait_recv()
            value = value + sums[n, token_rows(slot), :].astype(F32)
        out[:, columns(n)] = value.astype(BF16)

    for j in range(1, NZ):
        meta_copy(j).start()
    for f in range(GATHER_AHEAD):
        gather_start(f)
    for k in range(3):
        weight_local(k).start()
        weight_remote(k).start()

    def within(f, do):
        @pl.when(jnp.logical_and(f >= 0, f < chunks))
        def _():
            do(f)

    def out_step(t, carry):
        within(t + GATHER_AHEAD, gather_start)
        within(t, gather_second)
        within(t - 1, gather_third)
        within(t - 2, gather_fourth)

        @pl.when(t == 0)
        def _():
            acc[...] = jnp.zeros_like(acc)

        @pl.when(t == 1)
        def _():
            build_places()

        def pack_and_send(f):
            gather_last(f)
            pack(f)
            send_rows(f)

        within(t - 3, pack_and_send)

        @pl.when(t == 4)
        def _():
            build_spread()
            for k in range(3):
                weight_local(k).wait()
                weight_remote(k).wait_recv()

        def absorb(f):
            def one_block(b, carry):
                gate_up(f, b)
                return carry

            lax.fori_loop(0, PEERS // GROUP, one_block, 0)

        @pl.when(t - 3 - SEND_AHEAD >= 0)
        def _():
            absorb(t - 3 - SEND_AHEAD)

        return carry

    lax.fori_loop(0, chunks + 2 + SEND_AHEAD, out_step, 0)

    rows_sent(0)
    for b in range(PEERS // GROUP):
        gate_up(chunks - 1, b)
        activate(b)
        down(0, b)
        for i in range(b * GROUP, (b + 1) * GROUP):
            back_copy(0, i).start()
    for n in range(1, RETURN_AHEAD):
        down_and_send(n)

    def back_step(t, carry):
        within(t - 1, functools.partial(reduce_hop, k=2))
        within(t - 2, functools.partial(reduce_hop, k=3))
        within(t - 3, reduce_fourth)
        within(t - 4, reduce_last)
        within(t + RETURN_AHEAD, down_and_send)
        within(t, combine)
        return carry

    lax.fori_loop(0, chunks + 4, back_step, 0)

    for j in range(1, NZ):
        meta_copy(j).wait_send()
    for k in range(3):
        weight_remote(k).wait_send()

    def drain(n, carry):
        odd = lax.rem(n, 2)
        for j in range(1, NZ):
            ring_copy(n, j, j, up(1)).wait_send()
        for i in range(1, PEERS):
            back_copy(n, i).wait_send()
        for k in range(1, 4):
            sum_copy(n, 4 - k - odd, up(1)).wait_send()
            sum_copy(n, 4 + k - odd, up(1)).wait_send()
        sum_copy(n, 7 * odd, up(1)).wait_send()
        return carry

    lax.fori_loop(0, chunks, drain, 0)


def shards(width, tokens, expert_ids, gate_probs, w_gate, w_up, w_down):
    n_tok, d = tokens.shape
    half = w_down.shape[1]
    chunks = d // width
    weights = gate_probs / jnp.sum(gate_probs, axis=1, keepdims=True)
    meta = jnp.concatenate([expert_ids.astype(F32).T, weights.T], axis=0)
    dma = pltpu.SemaphoreType.DMA
    hbm = pl.BlockSpec(memory_space=pl.ANY)
    vmem = pl.BlockSpec(memory_space=pltpu.VMEM)
    return pl.pallas_call(
        kernel,
        out_shape=jax.ShapeDtypeStruct((n_tok, d), BF16),
        in_specs=[hbm, vmem, hbm, hbm, hbm],
        out_specs=vmem,
        scratch_shapes=[
            pltpu.VMEM((chunks, NZ * n_tok, width), BF16),
            pltpu.VMEM((NZ, 16, n_tok), F32),
            pltpu.VMEM((ALL, NZ * n_tok), BF16),
            pltpu.VMEM((NZ * n_tok, ALL), BF16),
            pltpu.VMEM((PEERS, NZ * n_tok), F32),
            pltpu.VMEM((PEERS, NZ * n_tok), F32),
            pltpu.VMEM((chunks, ALL, width), BF16),
            pltpu.VMEM((chunks, ALL, width), BF16),
            pltpu.VMEM((d, 4 * half), BF16),
            pltpu.VMEM((2 * half, d), BF16),
            pltpu.VMEM((SUMS, ALL, width), F32),
            pltpu.VMEM((ALL, 2 * half), BF16),
            pltpu.VMEM((chunks, ALL, width), BF16),
            pltpu.VMEM((chunks, NZ * n_tok, width), BF16),
            pltpu.VMEM((chunks, NZ * n_tok, width), BF16),
            dma((chunks,)),
            dma((NZ,)),
            dma((NZ,)),
            dma((3,)),
            dma((3,)),
            dma((3,)),
            dma((chunks, NZ)),
            dma((chunks, NZ)),
            dma((chunks, PEERS)),
            dma((chunks, PEERS)),
            dma((chunks, PEERS)),
            dma((chunks, NZ)),
            dma((chunks, NZ)),
        ],
        compiler_params=pltpu.CompilerParams(
            collective_id=1, has_side_effects=True, vmem_limit_bytes=60 * 1024 * 1024
        ),
        name="expert_layer",
    )(tokens, meta, w_gate, w_up, w_down)


def solution(mesh):
    return jax.shard_map(
        functools.partial(shards, 256),
        mesh=mesh,
        in_specs=(
            P(("ctx", "exp"), None),
            P(("ctx", "exp"), None),
            P(("ctx", "exp"), None),
            P(("ctx", "exp"), None, None),
            P(("ctx", "exp"), None, None),
            P(("ctx", "exp"), None, None),
        ),
        out_specs=P(("ctx", "exp"), None),
        check_vma=False,
    )
```

```python
import functools

import jax
import jax.numpy as jnp
from jax import lax
from jax.experimental import pallas as pl
from jax.experimental.pallas import tpu as pltpu
from jax.sharding import PartitionSpec as P

MESH = pl.DeviceIdType.MESH
F32 = jnp.float32
BF16 = jnp.bfloat16

NY, NX, NZ = 4, 4, 8
PEERS = NY * NX
CAP = 10
ROWS = NZ * CAP
ALL = PEERS * ROWS
GATHER_AHEAD = 1
SEND_AHEAD = 2
RETURN_AHEAD = 2
GROUP = 4
SUMS = 6
ORDER = (1, 4, 3, 12, 2, 8, 5, 15, 7, 13, 6, 9, 14, 11, 10)


def kernel(
    tok, ids, probs, w_gate, w_up, w_down, out,
    ring, metas, pick, spread, place, share, packed, came, w_in, w_out, acc, hidden, back, part, sums,
    tok_sem, meta_s, meta_r, wt_l, wt_s, wt_r, ring_s, ring_r, row_s, row_r, back_r, sum_s, sum_r,
):
    n_tok, d = tok.shape
    chunks, _, _, width = ring.shape
    half = w_down.shape[1]
    tiles = w_in.shape[1] // 256
    block = GROUP * ROWS
    ctx, exp = lax.axis_index("ctx"), lax.axis_index("exp")
    y, x = ctx // NX, lax.rem(ctx, NX)
    z, core = exp // 2, lax.rem(exp, 2)

    def up(j):
        return (ctx, lax.rem(z + j, NZ) * 2 + core)

    def ahead(i):
        return (lax.rem(y + i // NX, NY) * NX + lax.rem(x + i % NX, NX), exp)

    def behind(i):
        return (lax.rem(y + NY - i // NX, NY) * NX + lax.rem(x + NX - i % NX, NX), exp)

    sibling = (ctx, z * 2 + 1 - core)

    def rdma(src, dst, send, recv, to):
        return pltpu.make_async_remote_copy(
            src_ref=src, dst_ref=dst, send_sem=send, recv_sem=recv, device_id=to, device_id_type=MESH
        )

    def token_rows(j):
        return pl.ds(pl.multiple_of(j * n_tok, n_tok), n_tok)

    def peer_rows(i):
        return pl.ds(pl.multiple_of(i * ROWS, ROWS), ROWS)

    def peers(b):
        return pl.ds(pl.multiple_of(b * GROUP, GROUP), GROUP)

    def flat(value):
        return value.reshape(value.shape[0] * value.shape[1], value.shape[2])

    def columns(f):
        return pl.ds(pl.multiple_of(f * width, width), width)

    def own_tokens(f):
        return pltpu.make_async_copy(tok.at[:, columns(f)], ring.at[f, 0], tok_sem.at[f])

    for f in range(chunks):
        own_tokens(f).start()
    weight_parts = (
        (w_gate.at[0], w_in, (pl.ds(0, d), 0, half)),
        (w_up.at[0], w_in, (pl.ds(0, d), 2 * half, half)),
        (w_down.at[0], w_out, (None, 0, half)),
    )

    def weight_dst(k, other):
        _, ref, (rows, at, size) = weight_parts[k]
        at = at + other * half
        if rows is None:
            return ref.at[pl.ds(at, size)]
        return ref.at[rows, pl.ds(at, size)]

    def weight_local(k):
        return pltpu.make_async_copy(weight_parts[k][0], weight_dst(k, 0), wt_l.at[k])

    def weight_remote(k):
        return rdma(weight_parts[k][0], weight_dst(k, 1), wt_s.at[k], wt_r.at[k], sibling)

    barrier = pltpu.get_barrier_semaphore()
    for j in range(1, NZ):
        pl.semaphore_signal(barrier, inc=1, device_id=up(j), device_id_type=MESH)
    for i in range(1, PEERS):
        pl.semaphore_signal(barrier, inc=1, device_id=ahead(i), device_id_type=MESH)
    pl.semaphore_signal(barrier, inc=1, device_id=sibling, device_id_type=MESH)
    weights = probs[...] / jnp.sum(probs[...], axis=1, keepdims=True)
    same = lax.broadcasted_iota(jnp.int32, (n_tok, n_tok), 0) == lax.broadcasted_iota(jnp.int32, (n_tok, n_tok), 1)
    eye = jnp.where(same, 1.0, 0.0).astype(BF16)
    turn = (((0,), (0,)), ((), ()))
    metas[0, 0:8] = lax.dot_general(ids[...].astype(F32).astype(BF16), eye, turn, preferred_element_type=F32)
    metas[0, 8:16] = lax.dot_general(weights.astype(BF16), eye, turn, preferred_element_type=F32)
    acc[...] = jnp.zeros_like(acc)
    pl.semaphore_wait(barrier, NZ + PEERS - 1)

    def meta_copy(j):
        return rdma(metas.at[0], metas.at[j], meta_s.at[j], meta_r.at[j], up(NZ - j))

    def ring_copy(f, src, dst, to):
        return rdma(ring.at[f, src], ring.at[f, dst], ring_s.at[f, dst], ring_r.at[f, dst], to)

    def ring_wait(f, j):
        ring_copy(f, j, j, up(1)).wait_recv()

    def gather_start(f):
        own_tokens(f).wait()
        ring_copy(f, 0, 7, up(1)).start()
        ring_copy(f, 0, 1, up(NZ - 1)).start()

    def gather_second(f):
        ring_wait(f, 7)
        ring_copy(f, 7, 6, up(1)).start()
        ring_wait(f, 1)
        ring_copy(f, 1, 2, up(NZ - 1)).start()

    def gather_third(f):
        ring_wait(f, 6)
        ring_copy(f, 6, 5, up(1)).start()
        ring_wait(f, 2)
        ring_copy(f, 2, 3, up(NZ - 1)).start()

    def gather_fourth(f):
        odd = lax.rem(f + core, 2)
        ring_wait(f, 5)
        ring_wait(f, 3)
        ring_copy(f, 5 - 2 * odd, 4, up(1 + (NZ - 2) * odd)).start()

    def gather_last(f):
        ring_wait(f, 4)

    def build_places():
        for j in range(1, NZ):
            meta_copy(j).wait_recv()
        i = lax.broadcasted_iota(jnp.int32, (PEERS, n_tok), 0)
        row, col = lax.shift_right_logical(i, 2) + y, lax.bitwise_and(i, 3) + x
        owner = lax.bitwise_and(row, 3) * NX + lax.bitwise_and(col, 3)
        expert = (owner * NZ + z).astype(F32)
        earlier = (
            lax.broadcasted_iota(jnp.int32, (n_tok, n_tok), 0) < lax.broadcasted_iota(jnp.int32, (n_tok, n_tok), 1)
        ).astype(F32).astype(BF16)
        for j in range(NZ):
            named = jnp.zeros((PEERS, n_tok), F32)
            weight = jnp.zeros((PEERS, n_tok), F32)
            for k in range(8):
                hit = metas[j, k : k + 1, :] == expert
                named = named + jnp.where(hit, 1.0, 0.0)
                weight = weight + jnp.where(hit, metas[j, 8 + k : 9 + k, :], 0.0)
            rank = jnp.dot(named.astype(BF16), earlier, preferred_element_type=F32)
            place[:, j * n_tok : (j + 1) * n_tok] = jnp.where(named > 0.5, rank + float(j * CAP), -1.0)
            share[:, j * n_tok : (j + 1) * n_tok] = weight

        def one_peer(i, carry):
            slot = lax.broadcasted_iota(jnp.int32, (ROWS, NZ * n_tok), 0).astype(F32)
            hit = slot == place[pl.ds(i, 1), :]
            pick[peer_rows(i), :] = jnp.where(hit, 1.0, 0.0).astype(BF16)
            return carry

        lax.fori_loop(0, PEERS, one_peer, 0)

    def build_spread():
        lane = lax.broadcasted_iota(jnp.int32, (PEERS, ALL), 1)
        first = lax.broadcasted_iota(jnp.int32, (PEERS, ALL), 0) * ROWS
        inside = jnp.logical_and(lane >= first, lane < first + ROWS)
        widen = jnp.where(inside, 1.0, 0.0).astype(BF16)
        slot = jnp.sum(jnp.where(inside, (lane - first).astype(F32), 0.0), axis=0, keepdims=True)

        def one_block(j, carry):
            at = token_rows(j)
            dims = (((0,), (0,)), ((), ()))
            target = lax.dot_general(place[:, at].astype(BF16), widen, dims, preferred_element_type=F32)
            weight = lax.dot_general(share[:, at].astype(BF16), widen, dims, preferred_element_type=F32)
            spread[at, :] = jnp.where(target == slot, weight, 0.0).astype(BF16)
            return carry

        lax.fori_loop(0, NZ, one_block, 0)

    def pack(f):
        def one_block(b, carry):
            rows = pl.ds(pl.multiple_of(b * block, block), block)
            value = jnp.dot(pick[rows, :], flat(ring[f]), preferred_element_type=F32).astype(BF16)
            packed[f, peers(b)] = value.reshape(GROUP, ROWS, width)
            return carry

        lax.fori_loop(0, PEERS // GROUP, one_block, 0)

    def row_copy(f, i):
        if i == 0:
            return pltpu.make_async_copy(packed.at[f, i], came.at[f, i], row_r.at[f, i])
        return rdma(packed.at[f, i], came.at[f, i], row_s.at[f, i], row_r.at[f, i], ahead(i))

    def send_rows(f):
        for i in ORDER + (0,):
            row_copy(f, i).start()

    def gate_up(f, b):
        for i in range(GROUP):
            at = b * GROUP + i
            pltpu.make_async_copy(came.at[f, at], came.at[f, at], row_r.at[f, at]).wait()
        rows = pl.ds(pl.multiple_of(b * block, block), block)
        depth = pl.ds(pl.multiple_of(f * width, width), width)
        xs = flat(came[f, peers(b)])
        for t in range(tiles):
            acc[t, rows, :] += jnp.dot(xs, w_in[depth, t * 256 : (t + 1) * 256], preferred_element_type=F32)

    def activate(b):
        for q in range(GROUP):
            rows = peer_rows(b * GROUP + q)
            for t in range(tiles // 2):
                g, u = acc[t, rows, :], acc[tiles // 2 + t, rows, :]
                hidden[rows, t * 256 : (t + 1) * 256] = (g * (0.5 + 0.5 * jnp.tanh(0.5 * g)) * u).astype(BF16)

    def back_copy(n, i):
        if i == 0:
            return pltpu.make_async_copy(packed.at[n, i], back.at[n, i], back_r.at[n, i])
        return rdma(packed.at[n, i], back.at[n, i], row_s.at[n, i], back_r.at[n, i], behind(i))

    def rows_sent(n):
        for i in range(1, PEERS):
            row_copy(n, i).wait_send()

    def down(n, b):
        rows = pl.ds(pl.multiple_of(b * block, block), block)
        value = jnp.dot(hidden[rows, :], w_out[:, columns(n)], preferred_element_type=F32).astype(BF16)
        packed[n, peers(b)] = value.reshape(GROUP, ROWS, width)

    def down_and_send(n):
        rows_sent(n)

        def one_block(b, carry):
            down(n, b)
            return carry

        lax.fori_loop(0, PEERS // GROUP, one_block, 0)
        for i in ORDER + (0,):
            back_copy(n, i).start()

    def sum_copy(n, slot, to):
        return rdma(part.at[n, slot], sums.at[n, slot], sum_s.at[n, slot], sum_r.at[n, slot], to)

    def total(n, j):
        return acc[lax.rem(n, SUMS), token_rows(j), :]

    def pass_on(n, j, slot_in, slot_out, to):
        value = total(n, j)
        if slot_in is not None:
            sum_copy(n, slot_in, to).wait_recv()
            value = value + sums[n, slot_in].astype(F32)
        part[n, slot_out] = value.astype(BF16)
        sum_copy(n, slot_out, to).start()

    def combine(n):
        for i in range(PEERS):
            pltpu.make_async_copy(back.at[n, i], back.at[n, i], back_r.at[n, i]).wait()

        def one_block(j, carry):
            acc[lax.rem(n, SUMS), token_rows(j), :] = jnp.dot(
                spread[token_rows(j), :], flat(back[n]), preferred_element_type=F32
            )
            return carry

        lax.fori_loop(0, NZ, one_block, 0)
        odd = lax.rem(n + core, 2)
        pass_on(n, 4 - odd, None, 3 - odd, up(1))
        pass_on(n, 5 - odd, None, 5 - odd, up(NZ - 1))

    def reduce_hop(n, k):
        odd = lax.rem(n + core, 2)
        j = 5 - k - odd
        pass_on(n, j, j, j - 1, up(1))
        j = 4 + k - odd
        pass_on(n, j, j - 1, j, up(NZ - 1))

    def reduce_fourth(n):
        odd = lax.rem(n + core, 2)
        pass_on(n, 1 + 6 * odd, 1 + 5 * odd, 7 * odd, up(1 + (NZ - 2) * odd))

    def reduce_last(n):
        value = total(n, 0)
        for slot in (0, 7):
            sum_copy(n, slot, up(1)).wait_recv()
            value = value + sums[n, slot].astype(F32)
        out[:, columns(n)] = value.astype(BF16)

    gather_start(0)
    for j in range(1, NZ):
        meta_copy(j).start()
    for f in range(1, GATHER_AHEAD):
        gather_start(f)
    for k in range(3):
        weight_local(k).start()
        weight_remote(k).start()

    def within(f, do):
        @pl.when(jnp.logical_and(f >= 0, f < chunks))
        def _():
            do(f)

    def out_step(t, carry):
        within(t + GATHER_AHEAD, gather_start)
        within(t, gather_second)
        within(t - 1, gather_third)
        within(t - 2, gather_fourth)

        @pl.when(t == 1)
        def _():
            build_places()

        def pack_and_send(f):
            gather_last(f)
            pack(f)
            send_rows(f)

        within(t - 3, pack_and_send)

        @pl.when(t == 4)
        def _():
            build_spread()
            for k in range(3):
                weight_local(k).wait()
                weight_remote(k).wait_recv()

        def absorb(f):
            def one_block(b, carry):
                gate_up(f, b)
                return carry

            lax.fori_loop(0, PEERS // GROUP, one_block, 0)

        @pl.when(t - 3 - SEND_AHEAD >= 0)
        def _():
            absorb(t - 3 - SEND_AHEAD)

        return carry

    lax.fori_loop(0, chunks + 2 + SEND_AHEAD, out_step, 0)

    rows_sent(0)
    for b in range(PEERS // GROUP):
        gate_up(chunks - 1, b)
        activate(b)
        down(0, b)
        for i in range(b * GROUP, (b + 1) * GROUP):
            back_copy(0, i).start()
    for n in range(1, RETURN_AHEAD):
        down_and_send(n)

    def back_step(t, carry):
        within(t - 4, reduce_last)
        within(t - 3, reduce_fourth)
        within(t - 2, functools.partial(reduce_hop, k=3))
        within(t - 1, functools.partial(reduce_hop, k=2))
        within(t, combine)
        within(t + RETURN_AHEAD, down_and_send)
        return carry

    lax.fori_loop(0, chunks + 4, back_step, 0)

    for j in range(1, NZ):
        meta_copy(j).wait_send()
    for k in range(3):
        weight_remote(k).wait_send()

    def drain(n, carry):
        odd = lax.rem(n + core, 2)
        for j in range(1, NZ):
            ring_copy(n, j, j, up(1)).wait_send()
        for i in range(1, PEERS):
            back_copy(n, i).wait_send()
        for k in range(1, 4):
            sum_copy(n, 4 - k - odd, up(1)).wait_send()
            sum_copy(n, 4 + k - odd, up(1)).wait_send()
        sum_copy(n, 7 * odd, up(1)).wait_send()
        return carry

    lax.fori_loop(0, chunks, drain, 0)


def shards(width, tokens, expert_ids, gate_probs, w_gate, w_up, w_down):
    n_tok, d = tokens.shape
    half = w_down.shape[1]
    chunks = d // width
    dma = pltpu.SemaphoreType.DMA
    hbm = pl.BlockSpec(memory_space=pl.ANY)
    vmem = pl.BlockSpec(memory_space=pltpu.VMEM)
    return pl.pallas_call(
        kernel,
        out_shape=jax.ShapeDtypeStruct((n_tok, d), BF16),
        in_specs=[hbm, vmem, vmem, hbm, hbm, hbm],
        out_specs=vmem,
        scratch_shapes=[
            pltpu.VMEM((chunks, NZ, n_tok, width), BF16),
            pltpu.VMEM((NZ, 16, n_tok), F32),
            pltpu.VMEM((ALL, NZ * n_tok), BF16),
            pltpu.VMEM((NZ * n_tok, ALL), BF16),
            pltpu.VMEM((PEERS, NZ * n_tok), F32),
            pltpu.VMEM((PEERS, NZ * n_tok), F32),
            pltpu.VMEM((chunks, PEERS, ROWS, width), BF16),
            pltpu.VMEM((chunks, PEERS, ROWS, width), BF16),
            pltpu.VMEM((d, 4 * half), BF16),
            pltpu.VMEM((2 * half, d), BF16),
            pltpu.VMEM((SUMS, ALL, width), F32),
            pltpu.VMEM((ALL, 2 * half), BF16),
            pltpu.VMEM((chunks, PEERS, ROWS, width), BF16),
            pltpu.VMEM((chunks, NZ, n_tok, width), BF16),
            pltpu.VMEM((chunks, NZ, n_tok, width), BF16),
            dma((chunks,)),
            dma((NZ,)),
            dma((NZ,)),
            dma((3,)),
            dma((3,)),
            dma((3,)),
            dma((chunks, NZ)),
            dma((chunks, NZ)),
            dma((chunks, PEERS)),
            dma((chunks, PEERS)),
            dma((chunks, PEERS)),
            dma((chunks, NZ)),
            dma((chunks, NZ)),
        ],
        compiler_params=pltpu.CompilerParams(
            collective_id=1, has_side_effects=True, vmem_limit_bytes=60 * 1024 * 1024
        ),
        name="expert_layer",
    )(tokens, expert_ids, gate_probs, w_gate, w_up, w_down)


def solution(mesh):
    return jax.shard_map(
        functools.partial(shards, 256),
        mesh=mesh,
        in_specs=(
            P(("ctx", "exp"), None),
            P(("ctx", "exp"), None),
            P(("ctx", "exp"), None),
            P(("ctx", "exp"), None, None),
            P(("ctx", "exp"), None, None),
            P(("ctx", "exp"), None, None),
        ),
        out_specs=P(("ctx", "exp"), None),
        check_vma=False,
    )
```

```python
import functools

import jax
import jax.numpy as jnp
from jax import lax
from jax.experimental import pallas as pl
from jax.experimental.pallas import tpu as pltpu
from jax.sharding import PartitionSpec as P

MESH = pl.DeviceIdType.MESH
F32 = jnp.float32
BF16 = jnp.bfloat16

NY, NX, NZ = 4, 4, 8
PEERS = NY * NX
CAP = 10
ROWS = NZ * CAP
ALL = PEERS * ROWS
GATHER_AHEAD = 1
SEND_AHEAD = 2
RETURN_AHEAD = 2
GROUP = 4
SUMS = 6
ORDER = (1, 4, 3, 12, 2, 8, 5, 15, 7, 13, 6, 9, 14, 11, 10)


def kernel(
    tok, ids, probs, w_gate, w_up, w_down, out,
    ring, metas, pick, spread, place, share, packed, came, w_in, w_out, acc, hidden, back, part, sums,
    tok_sem, meta_s, meta_r, wt_l, wt_s, wt_r, ring_s, ring_r, row_s, row_r, back_r, sum_s, sum_r,
):
    n_tok, d = tok.shape
    chunks, _, _, width = ring.shape
    half = w_down.shape[1]
    tiles = w_in.shape[1] // 256
    block = GROUP * ROWS
    ctx, exp = lax.axis_index("ctx"), lax.axis_index("exp")
    y, x = ctx // NX, lax.rem(ctx, NX)
    z, core = exp // 2, lax.rem(exp, 2)

    def up(j):
        return (ctx, lax.rem(z + j, NZ) * 2 + core)

    def ahead(i):
        return (lax.rem(y + i // NX, NY) * NX + lax.rem(x + i % NX, NX), exp)

    def behind(i):
        return (lax.rem(y + NY - i // NX, NY) * NX + lax.rem(x + NX - i % NX, NX), exp)

    sibling = (ctx, z * 2 + 1 - core)

    def rdma(src, dst, send, recv, to):
        return pltpu.make_async_remote_copy(
            src_ref=src, dst_ref=dst, send_sem=send, recv_sem=recv, device_id=to, device_id_type=MESH
        )

    def token_rows(j):
        return pl.ds(pl.multiple_of(j * n_tok, n_tok), n_tok)

    def peer_rows(i):
        return pl.ds(pl.multiple_of(i * ROWS, ROWS), ROWS)

    def peers(b):
        return pl.ds(pl.multiple_of(b * GROUP, GROUP), GROUP)

    def flat(value):
        return value.reshape(value.shape[0] * value.shape[1], value.shape[2])

    def columns(f):
        return pl.ds(pl.multiple_of(f * width, width), width)

    def own_tokens(f):
        return pltpu.make_async_copy(tok.at[:, columns(f)], ring.at[f, 0], tok_sem.at[f])

    for f in range(chunks):
        own_tokens(f).start()
    weight_parts = (
        (w_gate.at[0], w_in, (pl.ds(0, d), 0, half)),
        (w_up.at[0], w_in, (pl.ds(0, d), 2 * half, half)),
        (w_down.at[0], w_out, (None, 0, half)),
    )

    def weight_dst(k, other):
        _, ref, (rows, at, size) = weight_parts[k]
        at = at + other * half
        if rows is None:
            return ref.at[pl.ds(at, size)]
        return ref.at[rows, pl.ds(at, size)]

    def weight_local(k):
        return pltpu.make_async_copy(weight_parts[k][0], weight_dst(k, 0), wt_l.at[k])

    def weight_remote(k):
        return rdma(weight_parts[k][0], weight_dst(k, 1), wt_s.at[k], wt_r.at[k], sibling)

    barrier = pltpu.get_barrier_semaphore()
    for j in range(1, NZ):
        pl.semaphore_signal(barrier, inc=1, device_id=up(j), device_id_type=MESH)
    for i in range(1, PEERS):
        pl.semaphore_signal(barrier, inc=1, device_id=ahead(i), device_id_type=MESH)
    pl.semaphore_signal(barrier, inc=1, device_id=sibling, device_id_type=MESH)
    metas[0, 0:8] = ids[...].astype(F32)
    metas[0, 8:16] = probs[...] / jnp.sum(probs[...], axis=0, keepdims=True)
    acc[...] = jnp.zeros_like(acc)
    pl.semaphore_wait(barrier, NZ + PEERS - 1)

    def meta_copy(j):
        return rdma(metas.at[0], metas.at[j], meta_s.at[j], meta_r.at[j], up(NZ - j))

    def ring_copy(f, src, dst, to):
        return rdma(ring.at[f, src], ring.at[f, dst], ring_s.at[f, dst], ring_r.at[f, dst], to)

    def ring_wait(f, j):
        ring_copy(f, j, j, up(1)).wait_recv()

    def gather_start(f):
        own_tokens(f).wait()
        ring_copy(f, 0, 7, up(1)).start()
        ring_copy(f, 0, 1, up(NZ - 1)).start()

    def gather_second(f):
        ring_wait(f, 7)
        ring_copy(f, 7, 6, up(1)).start()
        ring_wait(f, 1)
        ring_copy(f, 1, 2, up(NZ - 1)).start()

    def gather_third(f):
        ring_wait(f, 6)
        ring_copy(f, 6, 5, up(1)).start()
        ring_wait(f, 2)
        ring_copy(f, 2, 3, up(NZ - 1)).start()

    def gather_fourth(f):
        odd = lax.rem(f + core, 2)
        ring_wait(f, 5)
        ring_wait(f, 3)
        ring_copy(f, 5 - 2 * odd, 4, up(1 + (NZ - 2) * odd)).start()

    def gather_last(f):
        ring_wait(f, 4)

    def build_places():
        for j in range(1, NZ):
            meta_copy(j).wait_recv()
        i = lax.broadcasted_iota(jnp.int32, (PEERS, n_tok), 0)
        row, col = lax.shift_right_logical(i, 2) + y, lax.bitwise_and(i, 3) + x
        owner = lax.bitwise_and(row, 3) * NX + lax.bitwise_and(col, 3)
        expert = (owner * NZ + z).astype(F32)
        earlier = (
            lax.broadcasted_iota(jnp.int32, (n_tok, n_tok), 0) < lax.broadcasted_iota(jnp.int32, (n_tok, n_tok), 1)
        ).astype(F32).astype(BF16)
        for j in range(NZ):
            named = jnp.zeros((PEERS, n_tok), F32)
            weight = jnp.zeros((PEERS, n_tok), F32)
            for k in range(8):
                hit = metas[j, k : k + 1, :] == expert
                named = named + jnp.where(hit, 1.0, 0.0)
                weight = weight + jnp.where(hit, metas[j, 8 + k : 9 + k, :], 0.0)
            rank = jnp.dot(named.astype(BF16), earlier, preferred_element_type=F32)
            place[:, j * n_tok : (j + 1) * n_tok] = jnp.where(named > 0.5, rank + float(j * CAP), -1.0)
            share[:, j * n_tok : (j + 1) * n_tok] = weight

        def one_peer(i, carry):
            slot = lax.broadcasted_iota(jnp.int32, (ROWS, NZ * n_tok), 0).astype(F32)
            hit = slot == place[pl.ds(i, 1), :]
            pick[peer_rows(i), :] = jnp.where(hit, 1.0, 0.0).astype(BF16)
            return carry

        lax.fori_loop(0, PEERS, one_peer, 0)

    def build_spread():
        lane = lax.broadcasted_iota(jnp.int32, (PEERS, ALL), 1)
        first = lax.broadcasted_iota(jnp.int32, (PEERS, ALL), 0) * ROWS
        inside = jnp.logical_and(lane >= first, lane < first + ROWS)
        widen = jnp.where(inside, 1.0, 0.0).astype(BF16)
        slot = jnp.sum(jnp.where(inside, (lane - first).astype(F32), 0.0), axis=0, keepdims=True)

        def one_block(j, carry):
            at = token_rows(j)
            dims = (((0,), (0,)), ((), ()))
            target = lax.dot_general(place[:, at].astype(BF16), widen, dims, preferred_element_type=F32)
            weight = lax.dot_general(share[:, at].astype(BF16), widen, dims, preferred_element_type=F32)
            spread[at, :] = jnp.where(target == slot, weight, 0.0).astype(BF16)
            return carry

        lax.fori_loop(0, NZ, one_block, 0)

    def pack(f):
        def one_block(b, carry):
            rows = pl.ds(pl.multiple_of(b * block, block), block)
            value = jnp.dot(pick[rows, :], flat(ring[f]), preferred_element_type=F32).astype(BF16)
            packed[f, peers(b)] = value.reshape(GROUP, ROWS, width)
            return carry

        lax.fori_loop(0, PEERS // GROUP, one_block, 0)

    def row_copy(f, i):
        if i == 0:
            return pltpu.make_async_copy(packed.at[f, i], came.at[f, i], row_r.at[f, i])
        return rdma(packed.at[f, i], came.at[f, i], row_s.at[f, i], row_r.at[f, i], ahead(i))

    def send_rows(f):
        for i in ORDER + (0,):
            row_copy(f, i).start()

    def gate_up(f, b):
        for i in range(GROUP):
            at = b * GROUP + i
            pltpu.make_async_copy(came.at[f, at], came.at[f, at], row_r.at[f, at]).wait()
        rows = pl.ds(pl.multiple_of(b * block, block), block)
        depth = pl.ds(pl.multiple_of(f * width, width), width)
        xs = flat(came[f, peers(b)])
        for t in range(tiles):
            acc[t, rows, :] += jnp.dot(xs, w_in[depth, t * 256 : (t + 1) * 256], preferred_element_type=F32)

    def activate(b):
        for q in range(GROUP):
            rows = peer_rows(b * GROUP + q)
            for t in range(tiles // 2):
                g, u = acc[t, rows, :], acc[tiles // 2 + t, rows, :]
                hidden[rows, t * 256 : (t + 1) * 256] = (g * (0.5 + 0.5 * jnp.tanh(0.5 * g)) * u).astype(BF16)

    def back_copy(n, i):
        if i == 0:
            return pltpu.make_async_copy(packed.at[n, i], back.at[n, i], back_r.at[n, i])
        return rdma(packed.at[n, i], back.at[n, i], row_s.at[n, i], back_r.at[n, i], behind(i))

    def rows_sent(n):
        for i in range(1, PEERS):
            row_copy(n, i).wait_send()

    def down(n, b):
        rows = pl.ds(pl.multiple_of(b * block, block), block)
        value = jnp.dot(hidden[rows, :], w_out[:, columns(n)], preferred_element_type=F32).astype(BF16)
        packed[n, peers(b)] = value.reshape(GROUP, ROWS, width)

    def down_and_send(n):
        rows_sent(n)

        def one_block(b, carry):
            down(n, b)
            return carry

        lax.fori_loop(0, PEERS // GROUP, one_block, 0)
        for i in ORDER + (0,):
            back_copy(n, i).start()

    def sum_copy(n, slot, to):
        return rdma(part.at[n, slot], sums.at[n, slot], sum_s.at[n, slot], sum_r.at[n, slot], to)

    def total(n, j):
        return acc[lax.rem(n, SUMS), token_rows(j), :]

    def pass_on(n, j, slot_in, slot_out, to):
        value = total(n, j)
        if slot_in is not None:
            sum_copy(n, slot_in, to).wait_recv()
            value = value + sums[n, slot_in].astype(F32)
        part[n, slot_out] = value.astype(BF16)
        sum_copy(n, slot_out, to).start()

    def combine(n):
        for i in range(PEERS):
            pltpu.make_async_copy(back.at[n, i], back.at[n, i], back_r.at[n, i]).wait()

        def one_block(j, carry):
            acc[lax.rem(n, SUMS), token_rows(j), :] = jnp.dot(
                spread[token_rows(j), :], flat(back[n]), preferred_element_type=F32
            )
            return carry

        lax.fori_loop(0, NZ, one_block, 0)
        odd = lax.rem(n + core, 2)
        pass_on(n, 4 - odd, None, 3 - odd, up(1))
        pass_on(n, 5 - odd, None, 5 - odd, up(NZ - 1))

    def reduce_hop(n, k):
        odd = lax.rem(n + core, 2)
        j = 5 - k - odd
        pass_on(n, j, j, j - 1, up(1))
        j = 4 + k - odd
        pass_on(n, j, j - 1, j, up(NZ - 1))

    def reduce_fourth(n):
        odd = lax.rem(n + core, 2)
        pass_on(n, 1 + 6 * odd, 1 + 5 * odd, 7 * odd, up(1 + (NZ - 2) * odd))

    def reduce_last(n):
        value = total(n, 0)
        for slot in (0, 7):
            sum_copy(n, slot, up(1)).wait_recv()
            value = value + sums[n, slot].astype(F32)
        out[:, columns(n)] = value.astype(BF16)

    gather_start(0)
    for j in range(1, NZ):
        meta_copy(j).start()
    for f in range(1, GATHER_AHEAD):
        gather_start(f)
    for k in range(3):
        weight_local(k).start()
        weight_remote(k).start()

    def within(f, do):
        @pl.when(jnp.logical_and(f >= 0, f < chunks))
        def _():
            do(f)

    def out_step(t, carry):
        within(t + GATHER_AHEAD, gather_start)
        within(t, gather_second)
        within(t - 1, gather_third)
        within(t - 2, gather_fourth)

        @pl.when(t == 1)
        def _():
            build_places()

        def pack_and_send(f):
            gather_last(f)
            pack(f)
            send_rows(f)

        within(t - 3, pack_and_send)

        @pl.when(t == 4)
        def _():
            build_spread()
            for k in range(3):
                weight_local(k).wait()
                weight_remote(k).wait_recv()

        def absorb(f):
            def one_block(b, carry):
                gate_up(f, b)
                return carry

            lax.fori_loop(0, PEERS // GROUP, one_block, 0)

        @pl.when(t - 3 - SEND_AHEAD >= 0)
        def _():
            absorb(t - 3 - SEND_AHEAD)

        return carry

    lax.fori_loop(0, chunks + 2 + SEND_AHEAD, out_step, 0)

    rows_sent(0)
    for b in range(PEERS // GROUP):
        gate_up(chunks - 1, b)
        activate(b)
        down(0, b)
        for i in range(b * GROUP, (b + 1) * GROUP):
            back_copy(0, i).start()
    for n in range(1, RETURN_AHEAD):
        down_and_send(n)

    def back_step(t, carry):
        within(t - 4, reduce_last)
        within(t - 3, reduce_fourth)
        within(t - 2, functools.partial(reduce_hop, k=3))
        within(t - 1, functools.partial(reduce_hop, k=2))
        within(t, combine)
        within(t + RETURN_AHEAD, down_and_send)
        return carry

    lax.fori_loop(0, chunks + 4, back_step, 0)

    for j in range(1, NZ):
        meta_copy(j).wait_send()
    for k in range(3):
        weight_remote(k).wait_send()

    def drain(n, carry):
        odd = lax.rem(n + core, 2)
        for j in range(1, NZ):
            ring_copy(n, j, j, up(1)).wait_send()
        for i in range(1, PEERS):
            back_copy(n, i).wait_send()
        for k in range(1, 4):
            sum_copy(n, 4 - k - odd, up(1)).wait_send()
            sum_copy(n, 4 + k - odd, up(1)).wait_send()
        sum_copy(n, 7 * odd, up(1)).wait_send()
        return carry

    lax.fori_loop(0, chunks, drain, 0)


def shards(width, tokens, expert_ids, gate_probs, w_gate, w_up, w_down):
    n_tok, d = tokens.shape
    half = w_down.shape[1]
    chunks = d // width
    dma = pltpu.SemaphoreType.DMA
    hbm = pl.BlockSpec(memory_space=pl.ANY)
    vmem = pl.BlockSpec(memory_space=pltpu.VMEM)
    return pl.pallas_call(
        kernel,
        out_shape=jax.ShapeDtypeStruct((n_tok, d), BF16),
        in_specs=[hbm, vmem, vmem, hbm, hbm, hbm],
        out_specs=vmem,
        scratch_shapes=[
            pltpu.VMEM((chunks, NZ, n_tok, width), BF16),
            pltpu.VMEM((NZ, 16, n_tok), F32),
            pltpu.VMEM((ALL, NZ * n_tok), BF16),
            pltpu.VMEM((NZ * n_tok, ALL), BF16),
            pltpu.VMEM((PEERS, NZ * n_tok), F32),
            pltpu.VMEM((PEERS, NZ * n_tok), F32),
            pltpu.VMEM((chunks, PEERS, ROWS, width), BF16),
            pltpu.VMEM((chunks, PEERS, ROWS, width), BF16),
            pltpu.VMEM((d, 4 * half), BF16),
            pltpu.VMEM((2 * half, d), BF16),
            pltpu.VMEM((SUMS, ALL, width), F32),
            pltpu.VMEM((ALL, 2 * half), BF16),
            pltpu.VMEM((chunks, PEERS, ROWS, width), BF16),
            pltpu.VMEM((chunks, NZ, n_tok, width), BF16),
            pltpu.VMEM((chunks, NZ, n_tok, width), BF16),
            dma((chunks,)),
            dma((NZ,)),
            dma((NZ,)),
            dma((3,)),
            dma((3,)),
            dma((3,)),
            dma((chunks, NZ)),
            dma((chunks, NZ)),
            dma((chunks, PEERS)),
            dma((chunks, PEERS)),
            dma((chunks, PEERS)),
            dma((chunks, NZ)),
            dma((chunks, NZ)),
        ],
        compiler_params=pltpu.CompilerParams(
            collective_id=1, has_side_effects=True, vmem_limit_bytes=60 * 1024 * 1024
        ),
        name="expert_layer",
    )(tokens, expert_ids.T, gate_probs.T, w_gate, w_up, w_down)


def solution(mesh):
    return jax.shard_map(
        functools.partial(shards, 256),
        mesh=mesh,
        in_specs=(
            P(("ctx", "exp"), None),
            P(("ctx", "exp"), None),
            P(("ctx", "exp"), None),
            P(("ctx", "exp"), None, None),
            P(("ctx", "exp"), None, None),
            P(("ctx", "exp"), None, None),
        ),
        out_specs=P(("ctx", "exp"), None),
        check_vma=False,
    )
```

```python
import functools

import jax
import jax.numpy as jnp
from jax import lax
from jax.experimental import pallas as pl
from jax.experimental.pallas import tpu as pltpu
from jax.sharding import PartitionSpec as P

MESH = pl.DeviceIdType.MESH
F32 = jnp.float32
BF16 = jnp.bfloat16

NY, NX, NZ = 4, 4, 8
PEERS = NY * NX
CAP = 10
ROWS = NZ * CAP
ALL = PEERS * ROWS
GATHER_AHEAD = 1
SEND_AHEAD = 2
RETURN_AHEAD = 2
GROUP = 4
SUMS = 6
ORDER = (1, 4, 3, 12, 2, 8, 5, 15, 7, 13, 6, 9, 14, 11, 10)


def kernel(
    tok, ids, probs, w_gate, w_up, w_down, out,
    ring, metas, pick, spread, place, share, packed, came, w_in, w_out, acc, hidden, back, part, sums,
    tok_sem, meta_s, meta_r, wt_l, wt_s, wt_r, ring_s, ring_r, row_s, row_r, back_r, sum_s, sum_r,
):
    n_tok, d = tok.shape
    chunks, _, _, width = ring.shape
    half = w_down.shape[1]
    tiles = w_in.shape[1] // 256
    block = GROUP * ROWS
    ctx, exp = lax.axis_index("ctx"), lax.axis_index("exp")
    y, x = ctx // NX, lax.rem(ctx, NX)
    z, core = exp // 2, lax.rem(exp, 2)

    def up(j):
        return (ctx, lax.rem(z + j, NZ) * 2 + core)

    def ahead(i):
        return (lax.rem(y + i // NX, NY) * NX + lax.rem(x + i % NX, NX), exp)

    def behind(i):
        return (lax.rem(y + NY - i // NX, NY) * NX + lax.rem(x + NX - i % NX, NX), exp)

    sibling = (ctx, z * 2 + 1 - core)

    def rdma(src, dst, send, recv, to):
        return pltpu.make_async_remote_copy(
            src_ref=src, dst_ref=dst, send_sem=send, recv_sem=recv, device_id=to, device_id_type=MESH
        )

    def token_rows(j):
        return pl.ds(pl.multiple_of(j * n_tok, n_tok), n_tok)

    def peer_rows(i):
        return pl.ds(pl.multiple_of(i * ROWS, ROWS), ROWS)

    def peers(b):
        return pl.ds(pl.multiple_of(b * GROUP, GROUP), GROUP)

    def flat(value):
        return value.reshape(value.shape[0] * value.shape[1], value.shape[2])

    def columns(f):
        return pl.ds(pl.multiple_of(f * width, width), width)

    def own_tokens(f):
        return pltpu.make_async_copy(tok.at[:, columns(f)], ring.at[f, 0], tok_sem.at[f])

    for f in range(chunks):
        own_tokens(f).start()
    weight_parts = (
        (w_gate.at[0], w_in, (pl.ds(0, d), 0, half)),
        (w_up.at[0], w_in, (pl.ds(0, d), 2 * half, half)),
        (w_down.at[0], w_out, (None, 0, half)),
    )

    def weight_dst(k, other):
        _, ref, (rows, at, size) = weight_parts[k]
        at = at + other * half
        if rows is None:
            return ref.at[pl.ds(at, size)]
        return ref.at[rows, pl.ds(at, size)]

    def weight_local(k):
        return pltpu.make_async_copy(weight_parts[k][0], weight_dst(k, 0), wt_l.at[k])

    def weight_remote(k):
        return rdma(weight_parts[k][0], weight_dst(k, 1), wt_s.at[k], wt_r.at[k], sibling)

    barrier = pltpu.get_barrier_semaphore()
    for j in range(1, NZ):
        pl.semaphore_signal(barrier, inc=1, device_id=up(j), device_id_type=MESH)
    for i in range(1, PEERS):
        pl.semaphore_signal(barrier, inc=1, device_id=ahead(i), device_id_type=MESH)
    pl.semaphore_signal(barrier, inc=1, device_id=sibling, device_id_type=MESH)
    metas[0, 0:8] = ids[...].astype(F32)
    metas[0, 8:16] = probs[...] / jnp.sum(probs[...], axis=0, keepdims=True)
    acc[...] = jnp.zeros_like(acc)
    pl.semaphore_wait(barrier, NZ + PEERS - 1)

    def meta_copy(j):
        return rdma(metas.at[0], metas.at[j], meta_s.at[j], meta_r.at[j], up(NZ - j))

    def ring_copy(f, src, dst, to):
        return rdma(ring.at[f, src], ring.at[f, dst], ring_s.at[f, dst], ring_r.at[f, dst], to)

    def ring_wait(f, j):
        ring_copy(f, j, j, up(1)).wait_recv()

    def gather_start(f):
        own_tokens(f).wait()
        ring_copy(f, 0, 7, up(1)).start()
        ring_copy(f, 0, 1, up(NZ - 1)).start()

    def gather_second(f):
        ring_wait(f, 7)
        ring_copy(f, 7, 6, up(1)).start()
        ring_wait(f, 1)
        ring_copy(f, 1, 2, up(NZ - 1)).start()

    def gather_third(f):
        ring_wait(f, 6)
        ring_copy(f, 6, 5, up(1)).start()
        ring_wait(f, 2)
        ring_copy(f, 2, 3, up(NZ - 1)).start()

    def gather_fourth(f):
        odd = lax.rem(f + core, 2)
        ring_wait(f, 5)
        ring_wait(f, 3)
        ring_copy(f, 5 - 2 * odd, 4, up(1 + (NZ - 2) * odd)).start()

    def gather_last(f):
        ring_wait(f, 4)

    def build_places():
        for j in range(1, NZ):
            meta_copy(j).wait_recv()
        i = lax.broadcasted_iota(jnp.int32, (PEERS, n_tok), 0)
        row, col = lax.shift_right_logical(i, 2) + y, lax.bitwise_and(i, 3) + x
        owner = lax.bitwise_and(row, 3) * NX + lax.bitwise_and(col, 3)
        expert = (owner * NZ + z).astype(F32)
        earlier = (
            lax.broadcasted_iota(jnp.int32, (n_tok, n_tok), 0) < lax.broadcasted_iota(jnp.int32, (n_tok, n_tok), 1)
        ).astype(F32).astype(BF16)
        for j in range(NZ):
            named = jnp.zeros((PEERS, n_tok), F32)
            weight = jnp.zeros((PEERS, n_tok), F32)
            for k in range(8):
                hit = metas[j, k : k + 1, :] == expert
                named = named + jnp.where(hit, 1.0, 0.0)
                weight = weight + jnp.where(hit, metas[j, 8 + k : 9 + k, :], 0.0)
            rank = jnp.dot(named.astype(BF16), earlier, preferred_element_type=F32)
            place[:, j * n_tok : (j + 1) * n_tok] = jnp.where(named > 0.5, rank + float(j * CAP), -1.0)
            share[:, j * n_tok : (j + 1) * n_tok] = weight

        def one_peer(i, carry):
            slot = lax.broadcasted_iota(jnp.int32, (ROWS, NZ * n_tok), 0).astype(F32)
            hit = slot == place[pl.ds(i, 1), :]
            pick[peer_rows(i), :] = jnp.where(hit, 1.0, 0.0).astype(BF16)
            return carry

        lax.fori_loop(0, PEERS, one_peer, 0)

    def build_spread():
        lane = lax.broadcasted_iota(jnp.int32, (PEERS, ALL), 1)
        first = lax.broadcasted_iota(jnp.int32, (PEERS, ALL), 0) * ROWS
        inside = jnp.logical_and(lane >= first, lane < first + ROWS)
        widen = jnp.where(inside, 1.0, 0.0).astype(BF16)
        slot = jnp.sum(jnp.where(inside, (lane - first).astype(F32), 0.0), axis=0, keepdims=True)

        def one_block(j, carry):
            at = token_rows(j)
            dims = (((0,), (0,)), ((), ()))
            target = lax.dot_general(place[:, at].astype(BF16), widen, dims, preferred_element_type=F32)
            weight = lax.dot_general(share[:, at].astype(BF16), widen, dims, preferred_element_type=F32)
            spread[at, :] = jnp.where(target == slot, weight, 0.0).astype(BF16)
            return carry

        lax.fori_loop(0, NZ, one_block, 0)

    def pack(f):
        def one_block(b, carry):
            rows = pl.ds(pl.multiple_of(b * block, block), block)
            value = jnp.dot(pick[rows, :], flat(ring[f]), preferred_element_type=F32).astype(BF16)
            packed[f, peers(b)] = value.reshape(GROUP, ROWS, width)
            return carry

        lax.fori_loop(0, PEERS // GROUP, one_block, 0)

    def row_copy(f, i):
        if i == 0:
            return pltpu.make_async_copy(packed.at[f, i], came.at[f, i], row_r.at[f, i])
        return rdma(packed.at[f, i], came.at[f, i], row_s.at[f, i], row_r.at[f, i], ahead(i))

    def send_rows(f):
        for i in ORDER + (0,):
            row_copy(f, i).start()

    def gate_up(f, b):
        for i in range(GROUP):
            at = b * GROUP + i
            pltpu.make_async_copy(came.at[f, at], came.at[f, at], row_r.at[f, at]).wait()
        rows = pl.ds(pl.multiple_of(b * block, block), block)
        depth = pl.ds(pl.multiple_of(f * width, width), width)
        xs = flat(came[f, peers(b)])
        for t in range(tiles):
            acc[t, rows, :] += jnp.dot(xs, w_in[depth, t * 256 : (t + 1) * 256], preferred_element_type=F32)

    def activate(b):
        for q in range(GROUP):
            rows = peer_rows(b * GROUP + q)
            for t in range(tiles // 2):
                g, u = acc[t, rows, :], acc[tiles // 2 + t, rows, :]
                hidden[rows, t * 256 : (t + 1) * 256] = (g * (0.5 + 0.5 * jnp.tanh(0.5 * g)) * u).astype(BF16)

    def back_copy(n, i):
        if i == 0:
            return pltpu.make_async_copy(packed.at[n, i], back.at[n, i], back_r.at[n, i])
        return rdma(packed.at[n, i], back.at[n, i], row_s.at[n, i], back_r.at[n, i], behind(i))

    def rows_sent(n):
        for i in range(1, PEERS):
            row_copy(n, i).wait_send()

    def down(n, b):
        rows = pl.ds(pl.multiple_of(b * block, block), block)
        value = jnp.dot(hidden[rows, :], w_out[:, columns(n)], preferred_element_type=F32).astype(BF16)
        packed[n, peers(b)] = value.reshape(GROUP, ROWS, width)

    def down_and_send(n):
        rows_sent(n)

        def one_block(b, carry):
            down(n, b)
            return carry

        lax.fori_loop(0, PEERS // GROUP, one_block, 0)
        for i in ORDER + (0,):
            back_copy(n, i).start()

    def sum_copy(n, slot, to):
        return rdma(part.at[n, slot], sums.at[n, slot], sum_s.at[n, slot], sum_r.at[n, slot], to)

    def total(n, j):
        return acc[lax.rem(n, SUMS), token_rows(j), :]

    def pass_on(n, j, slot_in, slot_out, to):
        value = total(n, j)
        if slot_in is not None:
            sum_copy(n, slot_in, to).wait_recv()
            value = value + sums[n, slot_in].astype(F32)
        part[n, slot_out] = value.astype(BF16)
        sum_copy(n, slot_out, to).start()

    def combine(n):
        for i in range(PEERS):
            pltpu.make_async_copy(back.at[n, i], back.at[n, i], back_r.at[n, i]).wait()

        def one_block(j, carry):
            acc[lax.rem(n, SUMS), token_rows(j), :] = jnp.dot(
                spread[token_rows(j), :], flat(back[n]), preferred_element_type=F32
            )
            return carry

        lax.fori_loop(0, NZ, one_block, 0)
        odd = lax.rem(n + core, 2)
        pass_on(n, 4 - odd, None, 3 - odd, up(1))
        pass_on(n, 5 - odd, None, 5 - odd, up(NZ - 1))

    def reduce_hop(n, k):
        odd = lax.rem(n + core, 2)
        j = 5 - k - odd
        pass_on(n, j, j, j - 1, up(1))
        j = 4 + k - odd
        pass_on(n, j, j - 1, j, up(NZ - 1))

    def reduce_fourth(n):
        odd = lax.rem(n + core, 2)
        pass_on(n, 1 + 6 * odd, 1 + 5 * odd, 7 * odd, up(1 + (NZ - 2) * odd))

    def reduce_last(n):
        value = total(n, 0)
        for slot in (0, 7):
            sum_copy(n, slot, up(1)).wait_recv()
            value = value + sums[n, slot].astype(F32)
        out[:, columns(n)] = value.astype(BF16)

    gather_start(0)
    for j in range(1, NZ):
        meta_copy(j).start()
    for f in range(1, GATHER_AHEAD):
        gather_start(f)

    def within(f, do):
        @pl.when(jnp.logical_and(f >= 0, f < chunks))
        def _():
            do(f)

    def out_step(t, carry):
        within(t + GATHER_AHEAD, gather_start)
        within(t, gather_second)
        within(t - 1, gather_third)
        within(t - 2, gather_fourth)

        @pl.when(t == 1)
        def _():
            build_places()

        def pack_and_send(f):
            gather_last(f)
            pack(f)
            send_rows(f)

            @pl.when(f == 0)
            def _():
                for k in range(3):
                    weight_local(k).start()
                    weight_remote(k).start()

        within(t - 3, pack_and_send)

        @pl.when(t == 5)
        def _():
            build_spread()
            for k in range(3):
                weight_local(k).wait()
                weight_remote(k).wait_recv()

        def absorb(f):
            def one_block(b, carry):
                gate_up(f, b)
                return carry

            lax.fori_loop(0, PEERS // GROUP, one_block, 0)

        @pl.when(t - 3 - SEND_AHEAD >= 0)
        def _():
            absorb(t - 3 - SEND_AHEAD)

        return carry

    lax.fori_loop(0, chunks + 2 + SEND_AHEAD, out_step, 0)

    rows_sent(0)
    for b in range(PEERS // GROUP):
        gate_up(chunks - 1, b)
        activate(b)
        down(0, b)
        for i in range(b * GROUP, (b + 1) * GROUP):
            back_copy(0, i).start()
    for n in range(1, RETURN_AHEAD):
        down_and_send(n)

    def back_step(t, carry):
        within(t - 4, reduce_last)
        within(t - 3, reduce_fourth)
        within(t - 2, functools.partial(reduce_hop, k=3))
        within(t - 1, functools.partial(reduce_hop, k=2))
        within(t, combine)
        within(t + RETURN_AHEAD, down_and_send)
        return carry

    lax.fori_loop(0, chunks + 4, back_step, 0)

    for j in range(1, NZ):
        meta_copy(j).wait_send()
    for k in range(3):
        weight_remote(k).wait_send()

    def drain(n, carry):
        odd = lax.rem(n + core, 2)
        for j in range(1, NZ):
            ring_copy(n, j, j, up(1)).wait_send()
        for i in range(1, PEERS):
            back_copy(n, i).wait_send()
        for k in range(1, 4):
            sum_copy(n, 4 - k - odd, up(1)).wait_send()
            sum_copy(n, 4 + k - odd, up(1)).wait_send()
        sum_copy(n, 7 * odd, up(1)).wait_send()
        return carry

    lax.fori_loop(0, chunks, drain, 0)


def shards(width, tokens, expert_ids, gate_probs, w_gate, w_up, w_down):
    n_tok, d = tokens.shape
    half = w_down.shape[1]
    chunks = d // width
    dma = pltpu.SemaphoreType.DMA
    hbm = pl.BlockSpec(memory_space=pl.ANY)
    vmem = pl.BlockSpec(memory_space=pltpu.VMEM)
    return pl.pallas_call(
        kernel,
        out_shape=jax.ShapeDtypeStruct((n_tok, d), BF16),
        in_specs=[hbm, vmem, vmem, hbm, hbm, hbm],
        out_specs=vmem,
        scratch_shapes=[
            pltpu.VMEM((chunks, NZ, n_tok, width), BF16),
            pltpu.VMEM((NZ, 16, n_tok), F32),
            pltpu.VMEM((ALL, NZ * n_tok), BF16),
            pltpu.VMEM((NZ * n_tok, ALL), BF16),
            pltpu.VMEM((PEERS, NZ * n_tok), F32),
            pltpu.VMEM((PEERS, NZ * n_tok), F32),
            pltpu.VMEM((chunks, PEERS, ROWS, width), BF16),
            pltpu.VMEM((chunks, PEERS, ROWS, width), BF16),
            pltpu.VMEM((d, 4 * half), BF16),
            pltpu.VMEM((2 * half, d), BF16),
            pltpu.VMEM((SUMS, ALL, width), F32),
            pltpu.VMEM((ALL, 2 * half), BF16),
            pltpu.VMEM((chunks, PEERS, ROWS, width), BF16),
            pltpu.VMEM((chunks, NZ, n_tok, width), BF16),
            pltpu.VMEM((chunks, NZ, n_tok, width), BF16),
            dma((chunks,)),
            dma((NZ,)),
            dma((NZ,)),
            dma((3,)),
            dma((3,)),
            dma((3,)),
            dma((chunks, NZ)),
            dma((chunks, NZ)),
            dma((chunks, PEERS)),
            dma((chunks, PEERS)),
            dma((chunks, PEERS)),
            dma((chunks, NZ)),
            dma((chunks, NZ)),
        ],
        compiler_params=pltpu.CompilerParams(
            collective_id=1, has_side_effects=True, vmem_limit_bytes=60 * 1024 * 1024
        ),
        name="expert_layer",
    )(tokens, expert_ids.T, gate_probs.T, w_gate, w_up, w_down)


def solution(mesh):
    return jax.shard_map(
        functools.partial(shards, 256),
        mesh=mesh,
        in_specs=(
            P(("ctx", "exp"), None),
            P(("ctx", "exp"), None),
            P(("ctx", "exp"), None),
            P(("ctx", "exp"), None, None),
            P(("ctx", "exp"), None, None),
            P(("ctx", "exp"), None, None),
        ),
        out_specs=P(("ctx", "exp"), None),
        check_vma=False,
    )
```
